32 devices in a mesh: tile: 8 (over y, x, core), frame: 4 (over z).
Axes of the slice: x: 2, y: 2, z: 4, core: 2. Of those that a mesh axis runs over, the one named last changes fastest.
Arguments:
- frames: bfloat16 [8, 256, 512], P('frame', 'tile'), may hold values from -6 to 6
- row_shifts: int32 [512, 8], P('frame'), may hold values from -16 to 16, as said below
- column_shifts: int32 [512, 8], P('frame'), may hold values from -16 to 16, as said below
- frame_inverse_weight: float32 [8], replicated, may hold values from 0.05 to 0.5
- psf_rows: float32 [13], replicated, may hold values from 0.1 to 0.4
- psf_cols: float32 [13], replicated, may hold values from 0.1 to 0.4
Outputs:
- filtered: bfloat16 [512, 256, 512], P('frame', 'tile')
The draws below stay inside these ranges and needn't reach their ends.
Inputs may be any that keep to these rules, and one draw needn't show every extreme that they name: row_shifts[v, f] = floor(r_v * (2 f - 7) / 7) for an integer row rate r_v per velocity; both extremes are reached. column_shifts follows the same law with an integer column rate c_v per velocity; both extremes are reached; the rate pairs (r_v, c_v) are distinct across all 512 velocities.
All inputs are finite; a program needn't handle non-finite values.
Results may differ from the reference program's by a relative error of at most 0.005.
Values may be sent and summed in bfloat16 or wider, within the bound.
No kernel may reach another device: no remote copies, remote signals or barrier semaphores. Data moves between devices by JAX's collectives and lax.ppermute only.
A program may use at most 64 MiB of HBM per device.

```python
import math
import jax
import jax.numpy as jnp
from jax import lax

COLS = 512
FRAMES = 8
VELOCITIES = 512
HALO = 16
RADIUS = 6
TAPS = 13
HEIGHT = 256


def pair_codes(key):
    key = jax.random.fold_in(key, 17)
    side = 2 * HALO + 1
    total = side * side
    others = jax.random.permutation(key, jnp.arange(1, total - 1, dtype=jnp.int32))
    planted = jnp.array([total - 1, 0], dtype=jnp.int32)
    return jnp.concatenate([planted, others[:VELOCITIES - 2]])


def motion_table(speed):
    moments = 2 * jnp.arange(FRAMES, dtype=jnp.int32) - (FRAMES - 1)
    return speed[:, None] * moments[None, :] // (FRAMES - 1)


def draw_row_shifts(key, part):
    codes = pair_codes(key)
    return motion_table(codes // (2 * HALO + 1) - HALO)


def draw_column_shifts(key, part):
    codes = pair_codes(key)
    return motion_table(codes % (2 * HALO + 1) - HALO)


def steps_of(stream_key, shape, cuts, smallest, high):
    level, own = 1.0, jax.random.fold_in(stream_key, 6)
    for position, shards_of in cuts:
        heights = jnp.exp(jax.random.uniform(jax.random.fold_in(own, position), (shards_of,), jnp.float32, smallest / len(cuts), high / len(cuts)))
        level = level * jnp.repeat(heights, shape[position] // shards_of).reshape([-1 if axis == position else 1 for axis in range(len(shape))])
    return level


def bell_draw(rng, shape, spread, most, shards=(), kind=jnp.bfloat16):
    gain = steps_of(rng, shape, shards, -0.22, 0.18) if shards else 1.0
    values = jax.random.normal(rng, shape, jnp.float32) * spread * gain
    return jnp.minimum(jnp.maximum(values, -most), most).astype(kind)


def setup_inputs(seed: int = 0) -> dict:
    key_of = jax.random.split(jax.random.key(seed), 7)
    return {
        "frames": bell_draw(key_of[0], (FRAMES, HEIGHT, COLS), 1.0, 6.0, ((0, 4), (1, 8))),
        "row_shifts": draw_row_shifts(jax.random.fold_in(key_of[6], 71), 0),
        "column_shifts": draw_column_shifts(jax.random.fold_in(key_of[6], 71), 0),
        "frame_inverse_weight": jnp.clip(jnp.exp(jax.random.uniform(key_of[3], (FRAMES,), jnp.float32, math.log(0.05), math.log(0.5))), 0.05, 0.5),
        "psf_rows": jnp.clip(jax.random.uniform(key_of[4], (TAPS,), jnp.float32, 0.1, 0.4), 0.1, 0.4),
        "psf_cols": jnp.clip(jax.random.uniform(key_of[5], (TAPS,), jnp.float32, 0.1, 0.4), 0.1, 0.4),
    }


def reference(frames, row_shifts, column_shifts, frame_inverse_weight, psf_rows, psf_cols):
    image_height = frames.shape[1]
    width = frames.shape[2]
    padded = jnp.pad(frames, ((0, 0), (HALO, HALO), (HALO, HALO)))

    def one_velocity(offsets):
        row_moves, col_moves = offsets

        def add_frame(index, total):
            frame_image = lax.dynamic_index_in_dim(padded, index, 0, keepdims=False)
            row_start = (HALO + row_moves[index]).astype(jnp.int32)
            col_start = (HALO + col_moves[index]).astype(jnp.int32)
            moved = lax.dynamic_slice(frame_image, (row_start, col_start), (image_height, width))
            return total + frame_inverse_weight[index] * moved.astype(jnp.float32)

        summed = lax.fori_loop(0, FRAMES, add_frame, jnp.zeros((image_height, width), jnp.float32))
        stack = summed.astype(jnp.bfloat16)
        extended = jnp.pad(stack, ((RADIUS, RADIUS), (0, 0)))
        rowpass = jnp.zeros((image_height, width), jnp.float32)
        for k in range(2 * RADIUS + 1):
            rowpass = rowpass + psf_rows[k] * extended[k:k + image_height].astype(jnp.float32)
        wide_rows = jnp.pad(rowpass, ((0, 0), (RADIUS, RADIUS)))
        result = jnp.zeros((image_height, width), jnp.float32)
        for k in range(2 * RADIUS + 1):
            result = result + psf_cols[k] * wide_rows[:, k:k + width]
        return result.astype(jnp.bfloat16)

    return lax.map(one_velocity, (row_shifts, column_shifts))
```

```python
import functools

import jax
import jax.numpy as jnp
import numpy as np
from jax import lax
from jax.experimental import pallas as pl
from jax.experimental.pallas import tpu as pltpu
from jax.sharding import PartitionSpec as P

HALO = 16
RADIUS = 6
TAPS = 2 * RADIUS + 1
FRAMES = 8
RATES = 2 * HALO + 1
GROUP = 4
LANES = 128
FAR = 4096


def frame_moves(frame):
    return [rate * (2 * frame - (FRAMES - 1)) // (FRAMES - 1) for rate in range(-HALO, HALO + 1)]


LOWEST = [min(frame_moves(f)) for f in range(FRAMES)]
HIGHEST = [max(frame_moves(f)) for f in range(FRAMES)]
REACH = [(max(-LOWEST[f], HIGHEST[f]) + RADIUS + 1) // 2 * 2 for f in range(FRAMES)]
OFFSET = [sum(REACH[:f]) for f in range(FRAMES)]
SIDE = sum(REACH)
FIRST = [min(OFFSET[f] // 16, SIDE // 16 - 2) for f in range(FRAMES)]
ENTRIES = [(f, move) for f in range(FRAMES) for move in range(LOWEST[f], HIGHEST[f] + 1)]
BASE = [sum(HIGHEST[i] - LOWEST[i] + 1 for i in range(f)) for f in range(FRAMES)]


def rows_of_sum(rows):
    frame = [f for f in range(FRAMES) for _ in range(rows)]
    row = [y for _ in range(FRAMES) for y in range(rows)]
    for start in (None, rows):
        for f in range(FRAMES):
            frame += [f] * REACH[f]
            row += [(start if start is not None else -REACH[f]) + i for i in range(REACH[f])]
    return np.array(frame), np.array(row)


def prepare_kernel(velocities, slots, rows, height, place, row_moves, col_moves, taps_rows, taps_cols, lane_row, lane_moves,
                   weights_ref, band_ref, edge_ref, list_ref):
    start = place[0] * rows
    inside = lane_row[0:1, :]
    frame_row_ok = jnp.logical_and(inside + start >= 0, inside + start < height)
    y = lax.broadcasted_iota(jnp.int32, (rows, inside.shape[1]), 0)

    def one_rate(rate, _):
        stack_row = inside - lane_moves[pl.ds(rate, 1), :]
        ok = jnp.logical_and(frame_row_ok, jnp.logical_and(stack_row + start >= 0, stack_row + start < height))
        tap = jnp.where(ok, stack_row, FAR) - y
        value = jnp.zeros(tap.shape, jnp.float32)
        for k in range(TAPS):
            value = jnp.where(tap == k - RADIUS, taps_rows[k], value)
        weights_ref[rate] = value.astype(jnp.bfloat16)
        return 0

    lax.fori_loop(0, RATES, one_rate, 0)

    width, wide = band_ref.shape[0] // 2, band_ref.shape[1]
    for at in range(0, width, LANES):
        x = lax.broadcasted_iota(jnp.int32, (LANES, wide), 0) + at
        tap = x - (lax.broadcasted_iota(jnp.int32, (LANES, wide), 1) - HALO)
        value = jnp.zeros(tap.shape, jnp.float32)
        for k in range(TAPS):
            value = jnp.where(tap == k - RADIUS, taps_cols[k], value)
        high = value.astype(jnp.bfloat16)
        band_ref[at:at + LANES, :] = high
        band_ref[width + at:width + at + LANES, :] = (value - high.astype(jnp.float32)).astype(jnp.bfloat16)

    lane = lax.broadcasted_iota(jnp.int32, (LANES, LANES), 1)
    source = lax.broadcasted_iota(jnp.int32, (LANES, LANES), 0)
    move = lane // RADIUS + 1
    at = lane % RADIUS
    left = jnp.where(jnp.logical_and(source < move, move <= HALO), source - at - move, FAR)
    column = source - LANES
    right = jnp.where(jnp.logical_and(column >= -move, move <= HALO), column - (at - RADIUS) + move, FAR)
    for side, tap in enumerate((left, right)):
        value = jnp.zeros(tap.shape, jnp.float32)
        for k in range(TAPS):
            value = jnp.where(tap == k - RADIUS, taps_cols[k], value)
        high = value.astype(jnp.bfloat16)
        edge_ref[side, 0:LANES, :] = high
        edge_ref[side, LANES:, :] = (value - high.astype(jnp.float32)).astype(jnp.bfloat16)

    last = FRAMES - 1
    r_col = row_moves[:, last:last + 1] + HALO
    c_col = col_moves[:, last:last + 1] + HALO
    shape = (velocities, velocities)
    down = lax.broadcasted_iota(jnp.int32, shape, 0)
    across = lax.broadcasted_iota(jnp.int32, shape, 1)
    c_row = jnp.sum(jnp.where(down == across, c_col, 0), axis=0, keepdims=True)
    rank_row = jnp.sum(jnp.where(jnp.logical_and(c_col == c_row, down < across), 1, 0), axis=0, keepdims=True)
    rates = -(-RATES // 8) * 8
    rate_down = lax.broadcasted_iota(jnp.int32, (rates, velocities), 0)
    count_col = jnp.sum(jnp.where(rate_down == c_row, 1, 0), axis=1, keepdims=True)
    groups_col = (count_col + (GROUP - 1)) // GROUP
    before_row = jnp.sum(jnp.where(rate_down < c_row, groups_col, 0), axis=0, keepdims=True)
    slot_row = before_row * GROUP + rank_row
    slot_col = jnp.sum(jnp.where(down == across, slot_row, 0), axis=1, keepdims=True)
    slot_across = lax.broadcasted_iota(jnp.int32, (velocities, slots), 1)
    here = slot_col == slot_across
    which = lax.broadcasted_iota(jnp.int32, (velocities, slots), 0)
    list_ref[...] = jnp.zeros(list_ref.shape, jnp.int32)
    list_ref[0:1, :] = jnp.sum(jnp.where(here, which + 1, 0), axis=0, keepdims=True)
    list_ref[1:2, :] = jnp.sum(jnp.where(here, r_col, 0), axis=0, keepdims=True)
    list_ref[2:3, :] = jnp.sum(jnp.where(here, c_col, 0), axis=0, keepdims=True)
    total = jnp.sum(groups_col, axis=0, keepdims=True)
    list_ref[3:4, :] = jnp.broadcast_to(total, (1, slots))


def main_kernel(rows, width, pieces_count, place, lists, entries, entry_at, frame_weight, *refs):
    pieces = refs[:pieces_count]
    top, bottom, weights, band, edge, out, frames, filtered, outside, table, stage, sem = refs[pieces_count:]
    own = FRAMES // pieces_count
    middle = FRAMES * rows
    block = rows + 64

    for s, piece in enumerate(pieces):
        group = lax.rem(place[1] + pieces_count - s, pieces_count)
        for i in range(own):
            frames[pl.ds(pl.multiple_of((group * own + i) * rows, rows), rows), :] = piece[i]
    frames[middle:middle + SIDE, :] = top[...]
    frames[middle + SIDE:, :] = bottom[...]

    source = frames[...]
    spread = jnp.dot(source, band[:width, :], preferred_element_type=jnp.float32)
    spread += jnp.dot(source, band[width:, :], preferred_element_type=jnp.float32)
    ends = []
    for side, at in enumerate((0, width - LANES)):
        part = source[:, at:at + LANES]
        ends.append(jnp.dot(part, edge[side, :LANES, :], preferred_element_type=jnp.float32)
                    + jnp.dot(part, edge[side, LANES:, :], preferred_element_type=jnp.float32))
    ends = jnp.concatenate(ends, axis=1)
    for f in range(FRAMES):
        w = frame_weight[f]
        filtered[f, 0:rows, :] = (spread[f * rows:(f + 1) * rows] * w).astype(jnp.bfloat16)
        outside[f, 0:rows, :] = (ends[f * rows:(f + 1) * rows] * w).astype(jnp.bfloat16)
        for side in range(2):
            at = middle + side * SIDE + FIRST[f] * 16
            to = rows + 32 * side
            row = lax.broadcasted_iota(jnp.int32, (32, 1), 0) + FIRST[f] * 16
            scale = jnp.where(jnp.logical_and(row >= OFFSET[f], row < OFFSET[f] + REACH[f]), w, 0.0)
            filtered[f, to:to + 32, :] = (spread[at:at + 32] * scale).astype(jnp.bfloat16)
            outside[f, to:to + 32, :] = (ends[at:at + 32] * scale).astype(jnp.bfloat16)

    def one_entry(i, _):
        f = entries[0, i]
        moved = pltpu.roll(filtered[f], entries[1, i], 1)[:, :width]
        fix = outside[f]
        lane = lax.broadcasted_iota(jnp.int32, (block, LANES), 1)
        left = jnp.where(lane < RADIUS, pltpu.roll(fix[:, :LANES], entries[2, i], 1), 0)
        right = jnp.where(lane >= LANES - RADIUS, pltpu.roll(fix[:, LANES:], entries[3, i], 1), 0)
        table[i, :, :LANES] = moved[:, :LANES] - left
        table[i, :, LANES:width - LANES] = moved[:, LANES:width - LANES]
        table[i, :, width - LANES:] = moved[:, width - LANES:] - right
        return 0

    lax.fori_loop(0, len(ENTRIES), one_entry, 0)

    def one_group(k, _):
        c = lists[2, k * GROUP]
        at = [entry_at[f, c] for f in range(FRAMES)]
        parts = [table[at[f], 0:rows, :] for f in range(FRAMES)]
        for side in range(2):
            for tile in range(SIDE // 16):
                total = None
                for f in range(FRAMES):
                    for half in range(2):
                        low = (FIRST[f] + half) * 16
                        if FIRST[f] + half == tile and low < OFFSET[f] + REACH[f] and low + 16 > OFFSET[f]:
                            at_row = rows + 32 * side + 16 * half
                            piece = table[at[f], at_row:at_row + 16, :]
                            total = piece if total is None else total + piece
                parts.append(total)
        shifted = jnp.concatenate(parts, axis=0)
        chosen = jnp.concatenate([weights[lists[1, k * GROUP + i]] for i in range(GROUP)], axis=0)
        result = jnp.dot(chosen, shifted, preferred_element_type=jnp.float32).astype(jnp.bfloat16)
        for i in range(GROUP):
            v = lists[0, k * GROUP + i] - 1

            @pl.when(v >= 0)
            def _():
                stage[v] = result[i * rows:(i + 1) * rows]
                pltpu.make_async_copy(stage.at[v], out.at[v], sem).start()

        return 0

    lax.fori_loop(0, lists[3, 0], one_group, 0)
    pltpu.make_async_copy(stage, out, sem).wait()


def shards(frames, row_shifts, column_shifts, frame_inverse_weight, psf_rows, psf_cols):
    own, rows, width = frames.shape
    velocities = row_shifts.shape[0]
    groups = lax.axis_size("frame")
    bands = lax.axis_size("tile")
    height = bands * rows
    depth = FRAMES * rows + 2 * SIDE
    most = min(RATES, velocities)
    slots = -(-(velocities + (GROUP - 1) * most) // LANES) * LANES
    wide = width + LANES
    place = jnp.stack([lax.axis_index("tile"), lax.axis_index("frame")]).astype(jnp.int32)

    lane_frame, lane_row = rows_of_sum(rows)
    lane_moves = np.array([[frame_moves(f)[rate] for f in lane_frame] for rate in range(RATES)], np.int32)
    lane_moves = np.pad(lane_moves, ((0, -RATES % 8), (0, 0)))
    lane_rows = np.broadcast_to(lane_row.astype(np.int32), (8, depth))

    smem = pl.BlockSpec(memory_space=pltpu.SMEM)
    vmem = pl.BlockSpec(memory_space=pltpu.VMEM)
    weights, band, edge, lists = pl.pallas_call(
        functools.partial(prepare_kernel, velocities, slots, rows, height),
        out_shape=(
            jax.ShapeDtypeStruct((RATES, rows, depth), jnp.bfloat16),
            jax.ShapeDtypeStruct((2 * width, wide), jnp.bfloat16),
            jax.ShapeDtypeStruct((2, 2 * LANES, LANES), jnp.bfloat16),
            jax.ShapeDtypeStruct((8, slots), jnp.int32),
        ),
        in_specs=[smem, vmem, vmem, smem, smem, vmem, vmem],
        out_specs=(vmem, vmem, vmem, vmem),
        name="prepare",
    )(place, row_shifts, column_shifts, psf_rows, psf_cols, jnp.asarray(lane_rows), jnp.asarray(lane_moves))

    pieces = [frames]
    for s in range(1, groups):
        pieces.append(lax.ppermute(frames, "frame", [(i, (i + s) % groups) for i in range(groups)]))

    ordered = jnp.concatenate(pieces[::-1], axis=0)
    ordered = jnp.roll(ordered, (place[1] + 1) * own, axis=0)
    low = jnp.concatenate([ordered[f, rows - REACH[f]:] for f in range(FRAMES)], axis=0)
    high = jnp.concatenate([ordered[f, :REACH[f]] for f in range(FRAMES)], axis=0)
    top = lax.ppermute(low, "tile", [(i, (i + 1) % bands) for i in range(bands)])
    bottom = lax.ppermute(high, "tile", [((i + 1) % bands, i) for i in range(bands)])

    entries = np.zeros((8, -(-len(ENTRIES) // LANES) * LANES), np.int32)
    for i, (f, move) in enumerate(ENTRIES):
        entries[0, i] = f
        entries[1, i] = wide - (HALO + move)
        entries[2, i] = (LANES - RADIUS * (move - 1 if move > 0 else HALO)) % LANES
        entries[3, i] = (LANES - RADIUS - RADIUS * (-move - 1 if move < 0 else HALO)) % LANES
    entry_at = np.array([[BASE[f] + move - LOWEST[f] for move in frame_moves(f)] for f in range(FRAMES)], np.int32)
    entry_at = np.pad(entry_at, ((0, 0), (0, LANES - RATES)))

    block = rows + 64
    return pl.pallas_call(
        functools.partial(main_kernel, rows, width, groups),
        out_shape=jax.ShapeDtypeStruct((velocities, rows, width), jnp.bfloat16),
        in_specs=[smem] * 5 + [vmem] * (groups + 5),
        out_specs=pl.BlockSpec(memory_space=pl.ANY),
        scratch_shapes=[
            pltpu.VMEM((depth, width), jnp.bfloat16),
            pltpu.VMEM((FRAMES, block, wide), jnp.bfloat16),
            pltpu.VMEM((FRAMES, block, 2 * LANES), jnp.bfloat16),
            pltpu.VMEM((len(ENTRIES), block, width), jnp.bfloat16),
            pltpu.VMEM((velocities, rows, width), jnp.bfloat16),
            pltpu.SemaphoreType.DMA,
        ],
        compiler_params=pltpu.CompilerParams(vmem_limit_bytes=56 * 2**20),
        name="track",
    )(place, lists, jnp.asarray(entries), jnp.asarray(entry_at), frame_inverse_weight, *pieces, top, bottom, weights, band, edge)


def solution(mesh):
    return jax.shard_map(
        shards,
        mesh=mesh,
        in_specs=(P("frame", "tile", None), P("frame", None), P("frame", None), P(), P(), P()),
        out_specs=P("frame", "tile", None),
        check_vma=False,
    )
```
